32 devices in a mesh: rows: 8 (over z, y), cols: 4 (over x, core).
Axes of the slice: x: 2, y: 2, z: 4, core: 2. Of those that a mesh axis runs over, the one named last changes fastest.
Arguments:
- adjoint: float32 [3, 128, 384, 256], P(None, 'cols', 'rows'), may hold values from -6 to 6
- base_flow: bfloat16 [3, 128, 384, 256], P(None, 'cols', 'rows'), may hold values from -6 to 6
- stream_pair: bfloat16 [512, 256], replicated, may hold values from -0.375 to 0.375
- normal_pair: bfloat16 [768, 384], replicated, may hold values from -0.3125 to 0.3125
- span_pair: bfloat16 [256, 128], replicated, may hold values from -0.5 to 0.5
Outputs:
- adjoint_next: float32 [3, 128, 384, 256], P(None, 'cols', 'rows')
The draws below stay inside these ranges and needn't reach their ends.
All inputs are finite; a program needn't handle non-finite values.
Results may differ from the reference program's by a relative error of at most 0.0023.
Values may be sent and summed in bfloat16 or wider, within the bound.
A program may use at most 128 MiB of HBM per device.

```python
import jax
import jax.numpy as jnp
from jax import lax

NX = 256
NY = 384
NZ = 128


def shard_levels(own_key, extent, pieces, smallest, largest):
    level, own = 1.0, jax.random.fold_in(own_key, 6)
    for axis_at, blocks in pieces:
        heights = jnp.exp(jax.random.uniform(jax.random.fold_in(own, axis_at), (blocks,), jnp.float32, smallest / len(pieces), largest / len(pieces)))
        level = level * jnp.repeat(heights, extent[axis_at] // blocks).reshape([-1 if axis == axis_at else 1 for axis in range(len(extent))])
    return level


def bell_draw(stream_key, extent, scale, bound, cuts=(), held_as=jnp.bfloat16):
    values = jax.random.normal(stream_key, extent, jnp.float32) * scale
    if len(cuts) > 0:
        values = shard_levels(stream_key, extent, cuts, -0.22, 0.18) * values
    return jnp.clip(values, min=-bound, max=bound).astype(held_as)


def setup_inputs(seed: int = 0) -> dict:
    seeds = jax.random.split(jax.random.key(seed), 6)
    return {
        "adjoint": bell_draw(seeds[0], (3, NZ, NY, NX), 1.0, 6.0, ((1, 4), (2, 8)), jnp.float32),
        "base_flow": bell_draw(seeds[1], (3, NZ, NY, NX), 1.0, 6.0, ((1, 4), (2, 8))),
        "stream_pair": bell_draw(seeds[2], (2 * NX, NX), NX ** -0.5, 0.375),
        "normal_pair": bell_draw(seeds[3], (2 * NY, NY), NY ** -0.5, 0.3125),
        "span_pair": bell_draw(seeds[4], (2 * NZ, NZ), NZ ** -0.5, 0.5),
    }


viscosity = 0.5
section_step = 0.5


def direction_terms(lines, matrices, axis_index):
    length = lines.shape[3]
    adjoint_f = lines[:3].astype(jnp.float32)
    base_f = lines[3:].astype(jnp.float32)
    matrix_f = matrices.astype(jnp.float32)
    derivs = jnp.einsum("fabn,mn->fabm", adjoint_f, matrix_f, precision=lax.Precision.HIGHEST)
    first_deriv = derivs[..., :length]
    second = derivs[..., length:]
    base_deriv = jnp.einsum("fabn,mn->fabm", base_f, matrix_f[:length], precision=lax.Precision.HIGHEST)
    transfer = jnp.sum(adjoint_f * base_deriv, axis=0)
    result = base_f[axis_index][None] * first_deriv + viscosity * second
    listing = [result[component] - transfer if component == axis_index else result[component] for component in range(3)]
    return jnp.stack(listing)


def reference(adjoint, base_flow, stream_pair, normal_pair, span_pair):
    stacked = jnp.concatenate([adjoint.astype(jnp.bfloat16), base_flow.astype(jnp.bfloat16)], axis=0)

    def along_x(plane):
        return direction_terms(plane[:, None], stream_pair, 0)[:, 0]

    def along_y(plane):
        return direction_terms(plane[:, None], normal_pair, 1)[:, 0]

    def along_z(plane):
        return direction_terms(plane[:, None], span_pair, 2)[:, 0]

    terms_x = lax.map(along_x, stacked.transpose(1, 0, 2, 3)).transpose(1, 0, 2, 3)
    terms_y = lax.map(along_y, stacked.transpose(1, 0, 3, 2)).transpose(1, 0, 3, 2)
    terms_z = lax.map(along_z, stacked.transpose(2, 0, 3, 1)).transpose(1, 3, 0, 2)
    total = terms_x + terms_y + terms_z
    return adjoint + section_step * total
```

```python
import functools

import jax
import jax.numpy as jnp
from jax import lax
from jax.experimental import pallas as pl
from jax.experimental.pallas import tpu as pltpu
from jax.sharding import PartitionSpec as P

viscosity = 0.5
section_step = 0.5


def pack_lines(fields, pieces):
    count, outer, inner, length = fields.shape
    block = length // pieces
    split = fields.reshape(count, outer, inner, pieces, block)
    return split.transpose(0, 3, 1, 4, 2).reshape(count, pieces, outer, block * inner)


def unpack_lines(received, inner, outer_first):
    count, pieces, outer, merged = received.shape
    block = merged // inner
    split = received.reshape(count, pieces, outer, block, inner)
    if outer_first:
        return split.transpose(0, 2, 3, 1, 4).reshape(count, outer, block, pieces * inner)
    return split.transpose(0, 3, 2, 1, 4).reshape(count, block, outer, pieces * inner)


def direction_terms(lines, matrices, axis_index):
    length = lines.shape[3]
    adjoint_b = lines[:3]
    base_b = lines[3:]
    derivs = jnp.einsum("fabn,mn->fabm", adjoint_b, matrices, preferred_element_type=jnp.float32)
    first_deriv = derivs[..., :length]
    second = derivs[..., length:]
    base_deriv = jnp.einsum(
        "fabn,mn->fabm", base_b, matrices[:length], preferred_element_type=jnp.float32
    )
    adjoint_f = adjoint_b.astype(jnp.float32)
    base_f = base_b.astype(jnp.float32)
    transfer = jnp.sum(adjoint_f * base_deriv, axis=0)
    result = base_f[axis_index][None] * first_deriv + viscosity * second
    listing = [
        result[component] - transfer if component == axis_index else result[component]
        for component in range(3)
    ]
    return jnp.stack(listing)


def local(adjoint, base_flow, stream_pair, normal_pair, span_pair):
    row_count = lax.axis_size("rows")
    col_count = lax.axis_size("cols")
    stacked = jnp.concatenate([adjoint.astype(jnp.bfloat16), base_flow], axis=0)
    planes = stacked.shape[1]
    y_local = stacked.shape[2]
    terms_x = direction_terms(stacked, stream_pair, 0)

    def span_lines(portion):
        lines = unpack_lines(portion, planes, True)
        return direction_terms(lines, span_pair, 2)

    lines = unpack_lines(
        lax.all_to_all(
            pack_lines(stacked, row_count), "rows", split_axis=1, concat_axis=1, tiled=True
        ),
        y_local,
        False,
    )
    terms_y = direction_terms(lines, normal_pair, 1)
    terms_z = span_lines(
        lax.all_to_all(
            pack_lines(lines, col_count), "cols", split_axis=1, concat_axis=1, tiled=True
        )
    )
    returned = lax.all_to_all(
        pack_lines(terms_z, col_count), "cols", split_axis=1, concat_axis=1, tiled=True
    )
    gathered_y = terms_y + unpack_lines(returned, terms_z.shape[2], True)
    back = lax.all_to_all(
        pack_lines(gathered_y.transpose(0, 2, 1, 3), row_count),
        "rows",
        split_axis=1,
        concat_axis=1,
        tiled=True,
    )
    total = terms_x + unpack_lines(back, gathered_y.shape[1], True)
    return adjoint + section_step * total


def section_kernel(
    rows, cols, adjoint, base, stream_t, normal, span, out,
    a_bf, y_a, y_u, z_src, z_recv, y_term, y_back, z_term, z_back,
    ya_send, ya_recv, yu_send, yu_recv, yb_send, yb_recv, z_send, z_recv_sem, zb_send, zb_recv,
):
    row = lax.axis_index("rows")
    col = lax.axis_index("cols")
    _, nz, ny, nx = adjoint.shape
    zc = nz // rows
    yc = ny // cols

    def row_at(offset):
        return lax.rem(row + offset, rows)

    def col_at(offset):
        return lax.rem(col + offset, cols)

    barrier = pltpu.get_barrier_semaphore()
    for offset in range(1, rows):
        pl.semaphore_signal(
            barrier, inc=1, device_id={"rows": row_at(offset)}, device_id_type=pl.DeviceIdType.MESH
        )
    for offset in range(1, cols):
        pl.semaphore_signal(
            barrier, inc=1, device_id={"cols": col_at(offset)}, device_id_type=pl.DeviceIdType.MESH
        )
    pl.semaphore_wait(barrier, rows + cols - 2)

    def to_row(src, dst, send, recv, peer, chunk, source):
        return pltpu.make_async_remote_copy(
            src_ref=src, dst_ref=dst, send_sem=send.at[chunk, peer], recv_sem=recv.at[chunk, source],
            device_id={"rows": peer}, device_id_type=pl.DeviceIdType.MESH,
        )

    def to_col(src, dst, send, recv, peer, source):
        return pltpu.make_async_remote_copy(
            src_ref=src, dst_ref=dst, send_sem=send.at[peer], recv_sem=recv.at[source],
            device_id={"cols": peer}, device_id_type=pl.DeviceIdType.MESH,
        )

    def y_rows(index):
        return pl.ds(pl.multiple_of(index * ny, 16), ny)

    def z_rows(index):
        return pl.ds(pl.multiple_of(index * nz, 16), nz)

    def fwd_a(peer, chunk, source):
        return to_row(
            a_bf.at[:, peer * zc + chunk], y_a.at[:, chunk, y_rows(source)],
            ya_send, ya_recv, peer, chunk, source,
        )

    def fwd_u(peer, chunk, source):
        return to_row(
            base.at[:, peer * zc + chunk], y_u.at[:, chunk, y_rows(source)],
            yu_send, yu_recv, peer, chunk, source,
        )

    def back_y(peer, chunk, source):
        return to_row(
            y_term.at[:, chunk, y_rows(peer)], y_back.at[:, source * zc + chunk],
            yb_send, yb_recv, peer, chunk, source,
        )

    def fwd_z(peer, source):
        return to_col(
            z_src.at[:, pl.ds(peer * yc, yc)], z_recv.at[:, :, z_rows(source)],
            z_send, z_recv_sem, peer, source,
        )

    def back_z(peer, source):
        return to_col(
            z_term.at[:, :, z_rows(peer)], z_back.at[:, pl.ds(source * yc, yc)],
            zb_send, zb_recv, peer, source,
        )

    def row_loop(body):
        @pl.loop(1, rows)
        def _(offset):
            body(row_at(offset))

    def col_loop(body):
        @pl.loop(1, cols)
        def _(offset):
            body(col_at(offset))

    @pl.loop(0, nz)
    def _(z):
        a_bf[:, z] = adjoint[:, z].astype(jnp.bfloat16)

    @pl.loop(0, zc)
    def _(chunk):
        @pl.loop(1, rows)
        def _(offset):
            peer = row_at(offset)
            fwd_a(peer, chunk, row).start()
            fwd_u(peer, chunk, row).start()

    @pl.loop(0, 3)
    def _(field):
        for z0 in range(0, nz, 16):
            z_src[field, :, z0 : z0 + 16, :] = jnp.swapaxes(
                adjoint[field, z0 : z0 + 16], 0, 1
            ).astype(jnp.bfloat16)
            z_src[3 + field, :, z0 : z0 + 16, :] = jnp.swapaxes(
                base[field, z0 : z0 + 16].astype(jnp.float32), 0, 1
            ).astype(jnp.bfloat16)

    col_loop(lambda peer: fwd_z(peer, col).start())

    def terms(adj, flow, own, derive, length, axis):
        half = flow[own].astype(jnp.float32)
        transfer = None
        for field in range(3):
            part = adj[field].astype(jnp.float32) * derive(flow[field], False)
            transfer = part if transfer is None else transfer + part
        listing = []
        for field in range(3):
            both = derive(adj[field], True)
            first = lax.slice_in_dim(both, 0, length, axis=axis)
            second = lax.slice_in_dim(both, length, 2 * length, axis=axis)
            term = half * first + viscosity * second
            listing.append(term - transfer if field == own else term)
        return listing

    step = 4
    @pl.loop(0, nz // step)
    def _(part):
        planes = pl.ds(part * step, step)

        def derive(lines, both):
            matrix = stream_t[...] if both else stream_t[:, :nx]
            return jnp.dot(lines, matrix, preferred_element_type=jnp.float32)

        adj = [a_bf[field, planes].reshape(step * ny, nx) for field in range(3)]
        flow = [base[field, planes].reshape(step * ny, nx) for field in range(3)]
        for field, term in enumerate(terms(adj, flow, 0, derive, nx, 1)):
            out[field, planes] = adjoint[field, planes] + section_step * term.reshape(step, ny, nx)

    def column_terms(matrix_ref, adj, flow, own):
        length = matrix_ref.shape[1]

        def derive(lines, both):
            matrix = matrix_ref[...] if both else matrix_ref[:length]
            return jnp.dot(matrix, lines, preferred_element_type=jnp.float32)

        return terms(adj, flow, own, derive, length, 0)

    @pl.loop(0, zc)
    def _(chunk):
        for field in range(3):
            y_a[field, chunk, y_rows(row), :] = a_bf[field, row * zc + chunk]
            y_u[field, chunk, y_rows(row), :] = base[field, row * zc + chunk]

    @pl.loop(0, yc)
    def _(line):
        for field in range(6):
            z_recv[field, line, z_rows(col), :] = z_src[field, col * yc + line]

    def y_chunk(chunk):
        @pl.loop(1, rows)
        def _(offset):
            source = row_at(offset)
            fwd_a(source, chunk, source).wait_recv()
            fwd_u(source, chunk, source).wait_recv()

        adj = [y_a[field, chunk] for field in range(3)]
        flow = [y_u[field, chunk] for field in range(3)]
        for field, term in enumerate(column_terms(normal, adj, flow, 1)):
            y_term[field, chunk] = term.astype(jnp.bfloat16)

        @pl.loop(1, rows)
        def _(offset):
            back_y(row_at(offset), chunk, row).start()

        for field in range(3):
            out[field, row * zc + chunk] += section_step * y_term[
                field, chunk, y_rows(row), :
            ].astype(jnp.float32)

    early = zc // 2

    @pl.loop(0, early)
    def _(chunk):
        y_chunk(chunk)

    col_loop(lambda source: fwd_z(source, source).wait_recv())

    @pl.loop(0, yc)
    def _(line):
        adj = [z_recv[field, line] for field in range(3)]
        flow = [z_recv[3 + field, line] for field in range(3)]
        for field, term in enumerate(column_terms(span, adj, flow, 2)):
            z_term[field, line] = term.astype(jnp.bfloat16)

    col_loop(lambda peer: back_z(peer, col).start())

    @pl.loop(0, yc)
    def _(line):
        for field in range(3):
            z_back[field, col * yc + line] = z_term[field, line, z_rows(col), :]

    @pl.loop(early, zc)
    def _(chunk):
        y_chunk(chunk)

    col_loop(lambda source: back_z(source, source).wait_recv())

    @pl.loop(0, 3)
    def _(field):
        for z0 in range(0, nz, 16):
            out[field, z0 : z0 + 16] += section_step * jnp.swapaxes(
                z_back[field, :, z0 : z0 + 16, :].astype(jnp.float32), 0, 1
            )

    @pl.loop(0, zc)
    def _(chunk):
        @pl.loop(1, rows)
        def _(offset):
            source = row_at(offset)
            back_y(source, chunk, source).wait_recv()
            plane = source * zc + chunk
            out[:, plane] += section_step * y_back[:, plane].astype(jnp.float32)

    @pl.loop(0, zc)
    def _(chunk):
        @pl.loop(1, rows)
        def _(offset):
            peer = row_at(offset)
            fwd_a(peer, chunk, row).wait_send()
            fwd_u(peer, chunk, row).wait_send()
            back_y(peer, chunk, row).wait_send()

    @pl.loop(1, cols)
    def _(offset):
        peer = col_at(offset)
        fwd_z(peer, col).wait_send()
        back_z(peer, col).wait_send()


def local_kernel(adjoint, base_flow, stream_pair, normal_pair, span_pair):
    rows = lax.axis_size("rows")
    cols = lax.axis_size("cols")
    _, nz, ny, nx = adjoint.shape
    zc, yc = nz // rows, ny // cols
    bf = jnp.bfloat16
    vmem = pl.BlockSpec(memory_space=pltpu.VMEM)
    row_sems = [pltpu.SemaphoreType.DMA((zc, rows))] * 6
    col_sems = [pltpu.SemaphoreType.DMA((cols,))] * 4
    return pl.pallas_call(
        functools.partial(section_kernel, rows, cols),
        out_shape=jax.ShapeDtypeStruct(adjoint.shape, jnp.float32),
        in_specs=[vmem] * 5,
        out_specs=vmem,
        scratch_shapes=[
            pltpu.VMEM((3, nz, ny, nx), bf),
            pltpu.VMEM((3, zc, rows * ny, nx), bf),
            pltpu.VMEM((3, zc, rows * ny, nx), bf),
            pltpu.VMEM((6, ny, nz, nx), bf),
            pltpu.VMEM((6, yc, cols * nz, nx), bf),
            pltpu.VMEM((3, zc, rows * ny, nx), bf),
            pltpu.VMEM((3, nz, ny, nx), bf),
            pltpu.VMEM((3, yc, cols * nz, nx), bf),
            pltpu.VMEM((3, ny, nz, nx), bf),
            *row_sems,
            *col_sems,
        ],
        compiler_params=pltpu.CompilerParams(
            collective_id=0, has_side_effects=True, vmem_limit_bytes=60 * 1024 * 1024
        ),
    )(adjoint, base_flow, stream_pair.T, normal_pair, span_pair)


def section(adjoint, base_flow, stream_pair, normal_pair, span_pair):
    _, nz, ny, nx = adjoint.shape
    rows, cols = lax.axis_size("rows"), lax.axis_size("cols")
    whole = nz % 16 == 0 and ny % 16 == 0 and nx % 128 == 0
    if whole and nz % rows == 0 and ny % cols == 0:
        return local_kernel(adjoint, base_flow, stream_pair, normal_pair, span_pair)
    return local(adjoint, base_flow, stream_pair, normal_pair, span_pair)


def solution(mesh):
    placed = (P(None, "cols", "rows", None), P(None, "cols", "rows", None), P(), P(), P())
    return jax.shard_map(
        section, mesh=mesh, in_specs=placed, out_specs=P(None, "cols", "rows", None), check_vma=False
    )
```

```python
import functools

import jax
import jax.numpy as jnp
from jax import lax
from jax.experimental import pallas as pl
from jax.experimental.pallas import tpu as pltpu
from jax.sharding import PartitionSpec as P

viscosity = 0.5
section_step = 0.5


def pack_lines(fields, pieces):
    count, outer, inner, length = fields.shape
    block = length // pieces
    split = fields.reshape(count, outer, inner, pieces, block)
    return split.transpose(0, 3, 1, 4, 2).reshape(count, pieces, outer, block * inner)


def unpack_lines(received, inner, outer_first):
    count, pieces, outer, merged = received.shape
    block = merged // inner
    split = received.reshape(count, pieces, outer, block, inner)
    if outer_first:
        return split.transpose(0, 2, 3, 1, 4).reshape(count, outer, block, pieces * inner)
    return split.transpose(0, 3, 2, 1, 4).reshape(count, block, outer, pieces * inner)


def direction_terms(lines, matrices, axis_index):
    length = lines.shape[3]
    adjoint_b = lines[:3]
    base_b = lines[3:]
    derivs = jnp.einsum("fabn,mn->fabm", adjoint_b, matrices, preferred_element_type=jnp.float32)
    first_deriv = derivs[..., :length]
    second = derivs[..., length:]
    base_deriv = jnp.einsum(
        "fabn,mn->fabm", base_b, matrices[:length], preferred_element_type=jnp.float32
    )
    adjoint_f = adjoint_b.astype(jnp.float32)
    base_f = base_b.astype(jnp.float32)
    transfer = jnp.sum(adjoint_f * base_deriv, axis=0)
    result = base_f[axis_index][None] * first_deriv + viscosity * second
    listing = [
        result[component] - transfer if component == axis_index else result[component]
        for component in range(3)
    ]
    return jnp.stack(listing)


def local(adjoint, base_flow, stream_pair, normal_pair, span_pair):
    row_count = lax.axis_size("rows")
    col_count = lax.axis_size("cols")
    stacked = jnp.concatenate([adjoint.astype(jnp.bfloat16), base_flow], axis=0)
    planes = stacked.shape[1]
    y_local = stacked.shape[2]
    terms_x = direction_terms(stacked, stream_pair, 0)

    def span_lines(portion):
        lines = unpack_lines(portion, planes, True)
        return direction_terms(lines, span_pair, 2)

    lines = unpack_lines(
        lax.all_to_all(
            pack_lines(stacked, row_count), "rows", split_axis=1, concat_axis=1, tiled=True
        ),
        y_local,
        False,
    )
    terms_y = direction_terms(lines, normal_pair, 1)
    terms_z = span_lines(
        lax.all_to_all(
            pack_lines(lines, col_count), "cols", split_axis=1, concat_axis=1, tiled=True
        )
    )
    returned = lax.all_to_all(
        pack_lines(terms_z, col_count), "cols", split_axis=1, concat_axis=1, tiled=True
    )
    gathered_y = terms_y + unpack_lines(returned, terms_z.shape[2], True)
    back = lax.all_to_all(
        pack_lines(gathered_y.transpose(0, 2, 1, 3), row_count),
        "rows",
        split_axis=1,
        concat_axis=1,
        tiled=True,
    )
    total = terms_x + unpack_lines(back, gathered_y.shape[1], True)
    return adjoint + section_step * total


def section_kernel(
    rows, cols, adjoint_hbm, base_hbm, stream, normal, span, out_hbm, y_back,
    out, base, a_bf, y_a, y_u, z_src, z_recv, y_term, z_term, z_back,
    ya_send, ya_recv, yu_send, yu_recv, yb_send, yb_recv, z_send, z_recv_sem, zb_send, zb_recv,
    own_sem, load_sem,
):
    row = lax.axis_index("rows")
    col = lax.axis_index("cols")
    _, nz, ny, nx = out.shape
    zc = nz // rows
    yc = ny // cols
    half_rows = rows // 2
    own_half = row // half_rows

    load_adjoint = pltpu.make_async_copy(adjoint_hbm, out, load_sem.at[0])
    load_base = pltpu.make_async_copy(base_hbm, base, load_sem.at[1])
    load_adjoint.start()
    load_base.start()

    def row_at(offset):
        return lax.rem(row + offset, rows)

    def col_at(offset):
        return lax.rem(col + offset, cols)

    barrier = pltpu.get_barrier_semaphore()
    for offset in range(1, rows):
        pl.semaphore_signal(
            barrier, inc=1, device_id={"rows": row_at(offset)}, device_id_type=pl.DeviceIdType.MESH
        )
    for offset in range(1, cols):
        pl.semaphore_signal(
            barrier, inc=1, device_id={"cols": col_at(offset)}, device_id_type=pl.DeviceIdType.MESH
        )
    pl.semaphore_wait(barrier, rows + cols - 2)

    def to_row(src, dst, send, recv, peer, chunk, source):
        return pltpu.make_async_remote_copy(
            src_ref=src, dst_ref=dst, send_sem=send.at[chunk, peer], recv_sem=recv.at[chunk, source],
            device_id={"rows": peer}, device_id_type=pl.DeviceIdType.MESH,
        )

    def to_col(src, dst, send, recv, peer, source):
        return pltpu.make_async_remote_copy(
            src_ref=src, dst_ref=dst, send_sem=send.at[peer], recv_sem=recv.at[source],
            device_id={"cols": peer}, device_id_type=pl.DeviceIdType.MESH,
        )

    def y_rows(index):
        return pl.ds(pl.multiple_of(index * ny, 16), ny)

    def z_rows(index):
        return pl.ds(pl.multiple_of(index * nz, 16), nz)

    def fwd_a(peer, chunk, source):
        return to_row(
            a_bf.at[:, peer * zc + chunk], y_a.at[:, chunk, y_rows(source)],
            ya_send, ya_recv, peer, chunk, source,
        )

    def fwd_u(peer, chunk, source):
        return to_row(
            base_hbm.at[:, peer * zc + chunk], y_u.at[:, chunk, y_rows(source)],
            yu_send, yu_recv, peer, chunk, source,
        )

    def back_y(peer, chunk, source):
        return to_row(
            y_term.at[:, chunk, y_rows(peer)], y_back.at[:, source * zc + chunk],
            yb_send, yb_recv, peer, chunk, source,
        )

    def own_y(chunk):
        return pltpu.make_async_copy(
            y_term.at[:, chunk, y_rows(row)], y_back.at[:, row * zc + chunk], own_sem.at[chunk]
        )

    def fwd_z(peer, source):
        return to_col(
            z_src.at[:, pl.ds(peer * yc, yc)], z_recv.at[:, :, z_rows(source)],
            z_send, z_recv_sem, peer, source,
        )

    def back_z(peer, source):
        return to_col(
            z_term.at[:, :, z_rows(peer)], z_back.at[:, pl.ds(source * yc, yc)],
            zb_send, zb_recv, peer, source,
        )

    def row_loop(body):
        @pl.loop(0, half_rows)
        def _(offset):
            body((1 - own_half) * half_rows + lax.rem(row + offset, half_rows))

        @pl.loop(1, half_rows)
        def _(offset):
            body(own_half * half_rows + lax.rem(row + offset, half_rows))

    def col_loop(body):
        @pl.loop(1, cols)
        def _(offset):
            body(col_at(offset))

    row_loop(lambda peer: fwd_u(peer, 0, row).start())
    load_adjoint.wait()

    @pl.loop(0, nz)
    def _(z):
        a_bf[:, z] = out[:, z].astype(jnp.bfloat16)

    row_loop(lambda peer: fwd_a(peer, 0, row).start())

    @pl.loop(1, zc)
    def _(chunk):
        def both(peer):
            fwd_a(peer, chunk, row).start()
            fwd_u(peer, chunk, row).start()

        row_loop(both)

    load_base.wait()

    @pl.loop(0, 3)
    def _(field):
        for z0 in range(0, nz, 16):
            z_src[field, :, z0 : z0 + 16, :] = jnp.swapaxes(
                out[field, z0 : z0 + 16], 0, 1
            ).astype(jnp.bfloat16)
            z_src[3 + field, :, z0 : z0 + 16, :] = jnp.swapaxes(
                base[field, z0 : z0 + 16].astype(jnp.float32), 0, 1
            ).astype(jnp.bfloat16)

    col_loop(lambda peer: fwd_z(peer, col).start())

    def terms(adj, flow, own, derive, length, axis):
        half = flow[own].astype(jnp.float32)
        transfer = None
        for field in range(3):
            part = adj[field].astype(jnp.float32) * derive(flow[field], False)
            transfer = part if transfer is None else transfer + part
        listing = []
        for field in range(3):
            both = derive(adj[field], True)
            first = lax.slice_in_dim(both, 0, length, axis=axis)
            second = lax.slice_in_dim(both, length, 2 * length, axis=axis)
            term = half * first + viscosity * second
            listing.append(term - transfer if field == own else term)
        return listing

    step = 4
    @pl.loop(0, nz // step)
    def _(part):
        planes = pl.ds(part * step, step)

        def derive(lines, both):
            matrix = stream[...] if both else stream[:nx]
            return lax.dot_general(
                lines, matrix, (((1,), (1,)), ((), ())), preferred_element_type=jnp.float32
            )

        adj = [a_bf[field, planes].reshape(step * ny, nx) for field in range(3)]
        flow = [base[field, planes].reshape(step * ny, nx) for field in range(3)]
        for field, term in enumerate(terms(adj, flow, 0, derive, nx, 1)):
            out[field, planes] += section_step * term.reshape(step, ny, nx)

    def column_terms(matrix_ref, adj, flow, own):
        length = matrix_ref.shape[1]

        def derive(lines, both):
            matrix = matrix_ref[...] if both else matrix_ref[:length]
            return jnp.dot(matrix, lines, preferred_element_type=jnp.float32)

        return terms(adj, flow, own, derive, length, 0)

    @pl.loop(0, zc)
    def _(chunk):
        for field in range(3):
            y_a[field, chunk, y_rows(row), :] = a_bf[field, row * zc + chunk]
            y_u[field, chunk, y_rows(row), :] = base[field, row * zc + chunk]

    @pl.loop(0, yc)
    def _(line):
        for field in range(6):
            z_recv[field, line, z_rows(col), :] = z_src[field, col * yc + line]

    def y_chunk(chunk):
        @pl.loop(1, rows)
        def _(offset):
            source = row_at(offset)
            fwd_a(source, chunk, source).wait_recv()
            fwd_u(source, chunk, source).wait_recv()

        adj = [y_a[field, chunk] for field in range(3)]
        flow = [y_u[field, chunk] for field in range(3)]
        for field, term in enumerate(column_terms(normal, adj, flow, 1)):
            y_term[field, chunk] = term.astype(jnp.bfloat16)

        row_loop(lambda peer: back_y(peer, chunk, row).start())
        own_y(chunk).start()

    early = zc // 2

    @pl.loop(0, early)
    def _(chunk):
        y_chunk(chunk)

    col_loop(lambda source: fwd_z(source, source).wait_recv())

    @pl.loop(0, yc)
    def _(line):
        adj = [z_recv[field, line] for field in range(3)]
        flow = [z_recv[3 + field, line] for field in range(3)]
        for field, term in enumerate(column_terms(span, adj, flow, 2)):
            z_term[field, line] = term.astype(jnp.bfloat16)

    col_loop(lambda peer: back_z(peer, col).start())

    @pl.loop(0, yc)
    def _(line):
        for field in range(3):
            z_back[field, col * yc + line] = z_term[field, line, z_rows(col), :]

    @pl.loop(early, zc)
    def _(chunk):
        y_chunk(chunk)

    col_loop(lambda source: back_z(source, source).wait_recv())

    @pl.loop(0, 3)
    def _(field):
        for z0 in range(0, nz, 16):
            out[field, z0 : z0 + 16] += section_step * jnp.swapaxes(
                z_back[field, :, z0 : z0 + 16, :].astype(jnp.float32), 0, 1
            )

    store = pltpu.make_async_copy(out, out_hbm, load_sem.at[0])
    store.start()

    @pl.loop(0, zc)
    def _(chunk):
        own_y(chunk).wait()

        @pl.loop(1, rows)
        def _(offset):
            source = row_at(offset)
            back_y(source, chunk, source).wait_recv()

    store.wait()

    @pl.loop(0, zc)
    def _(chunk):
        @pl.loop(1, rows)
        def _(offset):
            peer = row_at(offset)
            fwd_a(peer, chunk, row).wait_send()
            fwd_u(peer, chunk, row).wait_send()
            back_y(peer, chunk, row).wait_send()

    @pl.loop(1, cols)
    def _(offset):
        peer = col_at(offset)
        fwd_z(peer, col).wait_send()
        back_z(peer, col).wait_send()


def local_kernel(adjoint, base_flow, stream_pair, normal_pair, span_pair):
    rows = lax.axis_size("rows")
    cols = lax.axis_size("cols")
    _, nz, ny, nx = adjoint.shape
    zc, yc = nz // rows, ny // cols
    bf = jnp.bfloat16
    vmem = pl.BlockSpec(memory_space=pltpu.VMEM)
    row_sems = [pltpu.SemaphoreType.DMA((zc, rows))] * 6
    col_sems = [pltpu.SemaphoreType.DMA((cols,))] * 4
    far = pl.BlockSpec(memory_space=pl.ANY)
    partial, y_terms = pl.pallas_call(
        functools.partial(section_kernel, rows, cols),
        out_shape=(
            jax.ShapeDtypeStruct(adjoint.shape, jnp.float32),
            jax.ShapeDtypeStruct(adjoint.shape, bf),
        ),
        in_specs=[far, far, vmem, vmem, vmem],
        out_specs=(far, far),
        scratch_shapes=[
            pltpu.VMEM((3, nz, ny, nx), jnp.float32),
            pltpu.VMEM((3, nz, ny, nx), bf),
            pltpu.VMEM((3, nz, ny, nx), bf),
            pltpu.VMEM((3, zc, rows * ny, nx), bf),
            pltpu.VMEM((3, zc, rows * ny, nx), bf),
            pltpu.VMEM((6, ny, nz, nx), bf),
            pltpu.VMEM((6, yc, cols * nz, nx), bf),
            pltpu.VMEM((3, zc, rows * ny, nx), bf),
            pltpu.VMEM((3, yc, cols * nz, nx), bf),
            pltpu.VMEM((3, ny, nz, nx), bf),
            *row_sems,
            *col_sems,
            pltpu.SemaphoreType.DMA((zc,)),
            pltpu.SemaphoreType.DMA((2,)),
        ],
        compiler_params=pltpu.CompilerParams(
            collective_id=0, has_side_effects=True, vmem_limit_bytes=60 * 1024 * 1024
        ),
    )(adjoint, base_flow, stream_pair, normal_pair, span_pair)
    return partial + section_step * y_terms.astype(jnp.float32)


def section(adjoint, base_flow, stream_pair, normal_pair, span_pair):
    _, nz, ny, nx = adjoint.shape
    rows, cols = lax.axis_size("rows"), lax.axis_size("cols")
    whole = nz % 16 == 0 and ny % 16 == 0 and nx % 128 == 0
    if whole and rows % 2 == 0 and nz % rows == 0 and ny % cols == 0:
        return local_kernel(adjoint, base_flow, stream_pair, normal_pair, span_pair)
    return local(adjoint, base_flow, stream_pair, normal_pair, span_pair)


def solution(mesh):
    placed = (P(None, "cols", "rows", None), P(None, "cols", "rows", None), P(), P(), P())
    return jax.shard_map(
        section, mesh=mesh, in_specs=placed, out_specs=P(None, "cols", "rows", None), check_vma=False
    )
```

```python
import functools

import jax
import jax.numpy as jnp
from jax import lax
from jax.experimental import pallas as pl
from jax.experimental.pallas import tpu as pltpu
from jax.sharding import PartitionSpec as P

viscosity = 0.5
section_step = 0.5


def pack_lines(fields, pieces):
    count, outer, inner, length = fields.shape
    block = length // pieces
    split = fields.reshape(count, outer, inner, pieces, block)
    return split.transpose(0, 3, 1, 4, 2).reshape(count, pieces, outer, block * inner)


def unpack_lines(received, inner, outer_first):
    count, pieces, outer, merged = received.shape
    block = merged // inner
    split = received.reshape(count, pieces, outer, block, inner)
    if outer_first:
        return split.transpose(0, 2, 3, 1, 4).reshape(count, outer, block, pieces * inner)
    return split.transpose(0, 3, 2, 1, 4).reshape(count, block, outer, pieces * inner)


def direction_terms(lines, matrices, axis_index):
    length = lines.shape[3]
    adjoint_b = lines[:3]
    base_b = lines[3:]
    derivs = jnp.einsum("fabn,mn->fabm", adjoint_b, matrices, preferred_element_type=jnp.float32)
    first_deriv = derivs[..., :length]
    second = derivs[..., length:]
    base_deriv = jnp.einsum(
        "fabn,mn->fabm", base_b, matrices[:length], preferred_element_type=jnp.float32
    )
    adjoint_f = adjoint_b.astype(jnp.float32)
    base_f = base_b.astype(jnp.float32)
    transfer = jnp.sum(adjoint_f * base_deriv, axis=0)
    result = base_f[axis_index][None] * first_deriv + viscosity * second
    listing = [
        result[component] - transfer if component == axis_index else result[component]
        for component in range(3)
    ]
    return jnp.stack(listing)


def local(adjoint, base_flow, stream_pair, normal_pair, span_pair):
    row_count = lax.axis_size("rows")
    col_count = lax.axis_size("cols")
    stacked = jnp.concatenate([adjoint.astype(jnp.bfloat16), base_flow], axis=0)
    planes = stacked.shape[1]
    y_local = stacked.shape[2]
    terms_x = direction_terms(stacked, stream_pair, 0)

    def span_lines(portion):
        lines = unpack_lines(portion, planes, True)
        return direction_terms(lines, span_pair, 2)

    lines = unpack_lines(
        lax.all_to_all(
            pack_lines(stacked, row_count), "rows", split_axis=1, concat_axis=1, tiled=True
        ),
        y_local,
        False,
    )
    terms_y = direction_terms(lines, normal_pair, 1)
    terms_z = span_lines(
        lax.all_to_all(
            pack_lines(lines, col_count), "cols", split_axis=1, concat_axis=1, tiled=True
        )
    )
    returned = lax.all_to_all(
        pack_lines(terms_z, col_count), "cols", split_axis=1, concat_axis=1, tiled=True
    )
    gathered_y = terms_y + unpack_lines(returned, terms_z.shape[2], True)
    back = lax.all_to_all(
        pack_lines(gathered_y.transpose(0, 2, 1, 3), row_count),
        "rows",
        split_axis=1,
        concat_axis=1,
        tiled=True,
    )
    total = terms_x + unpack_lines(back, gathered_y.shape[1], True)
    return adjoint + section_step * total


def section_kernel(
    rows, cols, adjoint_hbm, base_hbm, stream, normal, span, out_hbm, y_back,
    out, base, a_bf, y_a, y_u, z_src, z_recv, y_term, z_term, z_back,
    ya_send, ya_recv, yu_send, yu_recv, yb_send, yb_recv, z_send, z_recv_sem, zb_send, zb_recv,
    own_sem, load_sem,
):
    row = lax.axis_index("rows")
    col = lax.axis_index("cols")
    _, nz, ny, nx = out.shape
    zc = nz // rows
    yc = ny // cols
    yp = yc // zc
    half_rows = rows // 2
    own_half = row // half_rows

    load_adjoint = pltpu.make_async_copy(adjoint_hbm, out, load_sem.at[0])
    load_base = pltpu.make_async_copy(base_hbm, base, load_sem.at[1])
    load_adjoint.start()
    load_base.start()

    def row_at(offset):
        return lax.rem(row + offset, rows)

    def col_at(offset):
        return lax.rem(col + offset, cols)

    barrier = pltpu.get_barrier_semaphore()
    for offset in range(1, rows):
        pl.semaphore_signal(
            barrier, inc=1, device_id={"rows": row_at(offset)}, device_id_type=pl.DeviceIdType.MESH
        )
    for offset in range(1, cols):
        pl.semaphore_signal(
            barrier, inc=1, device_id={"cols": col_at(offset)}, device_id_type=pl.DeviceIdType.MESH
        )
    pl.semaphore_wait(barrier, rows + cols - 2)

    def to_row(src, dst, send, recv, peer, chunk, source):
        return pltpu.make_async_remote_copy(
            src_ref=src, dst_ref=dst, send_sem=send.at[chunk, peer], recv_sem=recv.at[chunk, source],
            device_id={"rows": peer}, device_id_type=pl.DeviceIdType.MESH,
        )

    def to_col(src, dst, send, recv, peer, part, source):
        return pltpu.make_async_remote_copy(
            src_ref=src, dst_ref=dst, send_sem=send.at[part, peer], recv_sem=recv.at[part, source],
            device_id={"cols": peer}, device_id_type=pl.DeviceIdType.MESH,
        )

    def y_rows(index):
        return pl.ds(pl.multiple_of(index * ny, 16), ny)

    def z_rows(index):
        return pl.ds(pl.multiple_of(index * nz, 16), nz)

    def fwd_a(peer, chunk, source):
        return to_row(
            a_bf.at[:, peer * zc + chunk], y_a.at[:, chunk, y_rows(source)],
            ya_send, ya_recv, peer, chunk, source,
        )

    def fwd_u(peer, chunk, source):
        return to_row(
            base_hbm.at[:, peer * zc + chunk], y_u.at[:, chunk, y_rows(source)],
            yu_send, yu_recv, peer, chunk, source,
        )

    def back_y(peer, chunk, source):
        return to_row(
            y_term.at[:, chunk, y_rows(peer)], y_back.at[:, source * zc + chunk],
            yb_send, yb_recv, peer, chunk, source,
        )

    def own_y(chunk):
        return pltpu.make_async_copy(
            y_term.at[:, chunk, y_rows(row)], y_back.at[:, row * zc + chunk], own_sem.at[chunk]
        )

    def fwd_z(peer, part, source):
        return to_col(
            z_src.at[:, pl.ds(peer * yc + part * yp, yp)],
            z_recv.at[:, pl.ds(part * yp, yp), z_rows(source)],
            z_send, z_recv_sem, peer, part, source,
        )

    def back_z(peer, part, source):
        return to_col(
            z_term.at[:, pl.ds(part * yp, yp), z_rows(peer)],
            z_back.at[:, pl.ds(source * yc + part * yp, yp)],
            zb_send, zb_recv, peer, part, source,
        )

    def row_loop(body):
        @pl.loop(0, half_rows)
        def _(offset):
            body((1 - own_half) * half_rows + lax.rem(row + offset, half_rows))

        @pl.loop(1, half_rows)
        def _(offset):
            body(own_half * half_rows + lax.rem(row + offset, half_rows))

    def col_loop(body):
        @pl.loop(1, cols)
        def _(offset):
            body(col_at(offset))

    row_loop(lambda peer: fwd_u(peer, 0, row).start())
    load_adjoint.wait()

    @pl.loop(0, nz)
    def _(z):
        a_bf[:, z] = out[:, z].astype(jnp.bfloat16)

    row_loop(lambda peer: fwd_a(peer, 0, row).start())

    load_base.wait()

    @pl.loop(0, 3)
    def _(field):
        for z0 in range(0, nz, 16):
            z_src[field, :, z0 : z0 + 16, :] = jnp.swapaxes(
                out[field, z0 : z0 + 16], 0, 1
            ).astype(jnp.bfloat16)
            z_src[3 + field, :, z0 : z0 + 16, :] = jnp.swapaxes(
                base[field, z0 : z0 + 16].astype(jnp.float32), 0, 1
            ).astype(jnp.bfloat16)

    @pl.loop(0, zc - 1)
    def _(chunk):
        def both(peer):
            fwd_a(peer, chunk + 1, row).start()
            fwd_u(peer, chunk + 1, row).start()

        col_loop(lambda peer: fwd_z(peer, chunk, col).start())
        row_loop(both)

    col_loop(lambda peer: fwd_z(peer, zc - 1, col).start())

    def terms(adj, flow, own, derive, length, axis):
        half = flow[own].astype(jnp.float32)
        transfer = None
        for field in range(3):
            part = adj[field].astype(jnp.float32) * derive(flow[field], False)
            transfer = part if transfer is None else transfer + part
        listing = []
        for field in range(3):
            both = derive(adj[field], True)
            first = lax.slice_in_dim(both, 0, length, axis=axis)
            second = lax.slice_in_dim(both, length, 2 * length, axis=axis)
            term = half * first + viscosity * second
            listing.append(term - transfer if field == own else term)
        return listing

    step = 4
    @pl.loop(0, nz // step)
    def _(part):
        planes = pl.ds(part * step, step)

        def derive(lines, both):
            matrix = stream[...] if both else stream[:nx]
            return lax.dot_general(
                lines, matrix, (((1,), (1,)), ((), ())), preferred_element_type=jnp.float32
            )

        adj = [a_bf[field, planes].reshape(step * ny, nx) for field in range(3)]
        flow = [base[field, planes].reshape(step * ny, nx) for field in range(3)]
        for field, term in enumerate(terms(adj, flow, 0, derive, nx, 1)):
            out[field, planes] += section_step * term.reshape(step, ny, nx)

    def column_terms(matrix_ref, adj, flow, own):
        length = matrix_ref.shape[1]

        def derive(lines, both):
            matrix = matrix_ref[...] if both else matrix_ref[:length]
            return jnp.dot(matrix, lines, preferred_element_type=jnp.float32)

        return terms(adj, flow, own, derive, length, 0)

    @pl.loop(0, zc)
    def _(chunk):
        for field in range(3):
            y_a[field, chunk, y_rows(row), :] = a_bf[field, row * zc + chunk]
            y_u[field, chunk, y_rows(row), :] = base[field, row * zc + chunk]

    @pl.loop(0, yc)
    def _(line):
        for field in range(6):
            z_recv[field, line, z_rows(col), :] = z_src[field, col * yc + line]

    def y_chunk(chunk):
        @pl.loop(1, rows)
        def _(offset):
            source = row_at(offset)
            fwd_a(source, chunk, source).wait_recv()
            fwd_u(source, chunk, source).wait_recv()

        adj = [y_a[field, chunk] for field in range(3)]
        flow = [y_u[field, chunk] for field in range(3)]
        for field, term in enumerate(column_terms(normal, adj, flow, 1)):
            y_term[field, chunk] = term.astype(jnp.bfloat16)

        row_loop(lambda peer: back_y(peer, chunk, row).start())
        own_y(chunk).start()

    def z_part(part):
        col_loop(lambda source: fwd_z(source, part, source).wait_recv())

        @pl.loop(0, yp)
        def _(step):
            line = part * yp + step
            adj = [z_recv[field, line] for field in range(3)]
            flow = [z_recv[3 + field, line] for field in range(3)]
            for field, term in enumerate(column_terms(span, adj, flow, 2)):
                z_term[field, line] = term.astype(jnp.bfloat16)

        col_loop(lambda peer: back_z(peer, part, col).start())

        @pl.loop(0, yp)
        def _(step):
            line = part * yp + step
            for field in range(3):
                z_back[field, col * yc + line] = z_term[field, line, z_rows(col), :]

    @pl.loop(0, zc)
    def _(chunk):
        y_chunk(chunk)
        z_part(chunk)

    @pl.loop(0, zc)
    def _(part):
        col_loop(lambda source: back_z(source, part, source).wait_recv())

    @pl.loop(0, 3)
    def _(field):
        for z0 in range(0, nz, 16):
            out[field, z0 : z0 + 16] += section_step * jnp.swapaxes(
                z_back[field, :, z0 : z0 + 16, :].astype(jnp.float32), 0, 1
            )

    store = pltpu.make_async_copy(out, out_hbm, load_sem.at[0])
    store.start()

    @pl.loop(0, zc)
    def _(chunk):
        own_y(chunk).wait()

        @pl.loop(1, rows)
        def _(offset):
            source = row_at(offset)
            back_y(source, chunk, source).wait_recv()

    store.wait()

    @pl.loop(0, zc)
    def _(chunk):
        @pl.loop(1, rows)
        def _(offset):
            peer = row_at(offset)
            fwd_a(peer, chunk, row).wait_send()
            fwd_u(peer, chunk, row).wait_send()
            back_y(peer, chunk, row).wait_send()

    @pl.loop(0, zc)
    def _(part):
        @pl.loop(1, cols)
        def _(offset):
            peer = col_at(offset)
            fwd_z(peer, part, col).wait_send()
            back_z(peer, part, col).wait_send()


def local_kernel(adjoint, base_flow, stream_pair, normal_pair, span_pair):
    rows = lax.axis_size("rows")
    cols = lax.axis_size("cols")
    _, nz, ny, nx = adjoint.shape
    zc, yc = nz // rows, ny // cols
    bf = jnp.bfloat16
    vmem = pl.BlockSpec(memory_space=pltpu.VMEM)
    row_sems = [pltpu.SemaphoreType.DMA((zc, rows))] * 6
    col_sems = [pltpu.SemaphoreType.DMA((zc, cols))] * 4
    far = pl.BlockSpec(memory_space=pl.ANY)
    partial, y_terms = pl.pallas_call(
        functools.partial(section_kernel, rows, cols),
        out_shape=(
            jax.ShapeDtypeStruct(adjoint.shape, jnp.float32),
            jax.ShapeDtypeStruct(adjoint.shape, bf),
        ),
        in_specs=[far, far, vmem, vmem, vmem],
        out_specs=(far, far),
        scratch_shapes=[
            pltpu.VMEM((3, nz, ny, nx), jnp.float32),
            pltpu.VMEM((3, nz, ny, nx), bf),
            pltpu.VMEM((3, nz, ny, nx), bf),
            pltpu.VMEM((3, zc, rows * ny, nx), bf),
            pltpu.VMEM((3, zc, rows * ny, nx), bf),
            pltpu.VMEM((6, ny, nz, nx), bf),
            pltpu.VMEM((6, yc, cols * nz, nx), bf),
            pltpu.VMEM((3, zc, rows * ny, nx), bf),
            pltpu.VMEM((3, yc, cols * nz, nx), bf),
            pltpu.VMEM((3, ny, nz, nx), bf),
            *row_sems,
            *col_sems,
            pltpu.SemaphoreType.DMA((zc,)),
            pltpu.SemaphoreType.DMA((2,)),
        ],
        compiler_params=pltpu.CompilerParams(
            collective_id=0, has_side_effects=True, vmem_limit_bytes=60 * 1024 * 1024
        ),
    )(adjoint, base_flow, stream_pair, normal_pair, span_pair)
    return partial + section_step * y_terms.astype(jnp.float32)


def section(adjoint, base_flow, stream_pair, normal_pair, span_pair):
    _, nz, ny, nx = adjoint.shape
    rows, cols = lax.axis_size("rows"), lax.axis_size("cols")
    whole = nz % 16 == 0 and ny % 16 == 0 and nx % 128 == 0
    if whole and rows % 2 == 0 and nz % rows == 0 and ny % (cols * (nz // rows)) == 0:
        return local_kernel(adjoint, base_flow, stream_pair, normal_pair, span_pair)
    return local(adjoint, base_flow, stream_pair, normal_pair, span_pair)


def solution(mesh):
    placed = (P(None, "cols", "rows", None), P(None, "cols", "rows", None), P(), P(), P())
    return jax.shard_map(
        section, mesh=mesh, in_specs=placed, out_specs=P(None, "cols", "rows", None), check_vma=False
    )
```

```python
import functools

import jax
import jax.numpy as jnp
from jax import lax
from jax.experimental import pallas as pl
from jax.experimental.pallas import tpu as pltpu
from jax.sharding import PartitionSpec as P

viscosity = 0.5
section_step = 0.5


def pack_lines(fields, pieces):
    count, outer, inner, length = fields.shape
    block = length // pieces
    split = fields.reshape(count, outer, inner, pieces, block)
    return split.transpose(0, 3, 1, 4, 2).reshape(count, pieces, outer, block * inner)


def unpack_lines(received, inner, outer_first):
    count, pieces, outer, merged = received.shape
    block = merged // inner
    split = received.reshape(count, pieces, outer, block, inner)
    if outer_first:
        return split.transpose(0, 2, 3, 1, 4).reshape(count, outer, block, pieces * inner)
    return split.transpose(0, 3, 2, 1, 4).reshape(count, block, outer, pieces * inner)


def direction_terms(lines, matrices, axis_index):
    length = lines.shape[3]
    adjoint_b = lines[:3]
    base_b = lines[3:]
    derivs = jnp.einsum("fabn,mn->fabm", adjoint_b, matrices, preferred_element_type=jnp.float32)
    first_deriv = derivs[..., :length]
    second = derivs[..., length:]
    base_deriv = jnp.einsum(
        "fabn,mn->fabm", base_b, matrices[:length], preferred_element_type=jnp.float32
    )
    adjoint_f = adjoint_b.astype(jnp.float32)
    base_f = base_b.astype(jnp.float32)
    transfer = jnp.sum(adjoint_f * base_deriv, axis=0)
    result = base_f[axis_index][None] * first_deriv + viscosity * second
    listing = [
        result[component] - transfer if component == axis_index else result[component]
        for component in range(3)
    ]
    return jnp.stack(listing)


def local(adjoint, base_flow, stream_pair, normal_pair, span_pair):
    row_count = lax.axis_size("rows")
    col_count = lax.axis_size("cols")
    stacked = jnp.concatenate([adjoint.astype(jnp.bfloat16), base_flow], axis=0)
    planes = stacked.shape[1]
    y_local = stacked.shape[2]
    terms_x = direction_terms(stacked, stream_pair, 0)

    def span_lines(portion):
        lines = unpack_lines(portion, planes, True)
        return direction_terms(lines, span_pair, 2)

    lines = unpack_lines(
        lax.all_to_all(
            pack_lines(stacked, row_count), "rows", split_axis=1, concat_axis=1, tiled=True
        ),
        y_local,
        False,
    )
    terms_y = direction_terms(lines, normal_pair, 1)
    terms_z = span_lines(
        lax.all_to_all(
            pack_lines(lines, col_count), "cols", split_axis=1, concat_axis=1, tiled=True
        )
    )
    returned = lax.all_to_all(
        pack_lines(terms_z, col_count), "cols", split_axis=1, concat_axis=1, tiled=True
    )
    gathered_y = terms_y + unpack_lines(returned, terms_z.shape[2], True)
    back = lax.all_to_all(
        pack_lines(gathered_y.transpose(0, 2, 1, 3), row_count),
        "rows",
        split_axis=1,
        concat_axis=1,
        tiled=True,
    )
    total = terms_x + unpack_lines(back, gathered_y.shape[1], True)
    return adjoint + section_step * total


def section_kernel(
    rows, cols, adjoint_hbm, base_hbm, stream, normal, span, out_hbm, y_back,
    out, base, a_bf, y_a, y_u, z_src, z_recv, y_term, z_term, z_back,
    ya_send, ya_recv, yu_send, yu_recv, yb_send, yb_recv, z_send, z_recv_sem, zb_send, zb_recv,
    own_sem, load_sem,
):
    row = lax.axis_index("rows")
    col = lax.axis_index("cols")
    _, nz, ny, nx = out.shape
    zc = nz // rows
    yc = ny // cols
    yp = yc // zc
    half_rows = rows // 2
    own_half = row // half_rows

    load_adjoint = pltpu.make_async_copy(adjoint_hbm, out, load_sem.at[0])
    load_base = pltpu.make_async_copy(base_hbm, base, load_sem.at[1])
    load_adjoint.start()
    load_base.start()

    def row_at(offset):
        return lax.rem(row + offset, rows)

    def col_at(offset):
        return lax.rem(col + offset, cols)

    barrier = pltpu.get_barrier_semaphore()
    for offset in range(1, rows):
        pl.semaphore_signal(
            barrier, inc=1, device_id={"rows": row_at(offset)}, device_id_type=pl.DeviceIdType.MESH
        )
    for offset in range(1, cols):
        pl.semaphore_signal(
            barrier, inc=1, device_id={"cols": col_at(offset)}, device_id_type=pl.DeviceIdType.MESH
        )
    pl.semaphore_wait(barrier, rows + cols - 2)

    def to_row(src, dst, send, recv, peer, chunk, source):
        return pltpu.make_async_remote_copy(
            src_ref=src, dst_ref=dst, send_sem=send.at[chunk, peer], recv_sem=recv.at[chunk, source],
            device_id={"rows": peer}, device_id_type=pl.DeviceIdType.MESH,
        )

    def to_col(src, dst, send, recv, peer, part, source):
        return pltpu.make_async_remote_copy(
            src_ref=src, dst_ref=dst, send_sem=send.at[part, peer], recv_sem=recv.at[part, source],
            device_id={"cols": peer}, device_id_type=pl.DeviceIdType.MESH,
        )

    def y_rows(index):
        return pl.ds(pl.multiple_of(index * ny, 16), ny)

    def z_rows(index):
        return pl.ds(pl.multiple_of(index * nz, 16), nz)

    def fwd_a(peer, chunk, source):
        return to_row(
            a_bf.at[:, peer * zc + chunk], y_a.at[:, chunk, y_rows(source)],
            ya_send, ya_recv, peer, chunk, source,
        )

    def fwd_u(peer, chunk, source):
        return to_row(
            base_hbm.at[:, peer * zc + chunk], y_u.at[:, chunk, y_rows(source)],
            yu_send, yu_recv, peer, chunk, source,
        )

    def back_y(peer, chunk, source):
        return to_row(
            y_term.at[:, chunk, y_rows(peer)], y_back.at[:, source * zc + chunk],
            yb_send, yb_recv, peer, chunk, source,
        )

    def own_y(chunk):
        return pltpu.make_async_copy(
            y_term.at[:, chunk, y_rows(row)], y_back.at[:, row * zc + chunk], own_sem.at[chunk]
        )

    def fwd_z(peer, part, source):
        return to_col(
            z_src.at[:, pl.ds(peer * yc + part * yp, yp)],
            z_recv.at[:, pl.ds(part * yp, yp), z_rows(source)],
            z_send, z_recv_sem, peer, part, source,
        )

    def back_z(peer, part, source):
        return to_col(
            z_term.at[:, pl.ds(part * yp, yp), z_rows(peer)],
            z_back.at[:, pl.ds(source * yc + part * yp, yp)],
            zb_send, zb_recv, peer, part, source,
        )

    def row_loop(body):
        @pl.loop(0, half_rows)
        def _(offset):
            body((1 - own_half) * half_rows + lax.rem(row + offset, half_rows))

        @pl.loop(1, half_rows)
        def _(offset):
            body(own_half * half_rows + lax.rem(row + offset, half_rows))

    def col_loop(body):
        @pl.loop(1, cols)
        def _(offset):
            body(col_at(offset))

    row_loop(lambda peer: fwd_u(peer, 0, row).start())
    load_adjoint.wait()

    @pl.loop(0, nz)
    def _(z):
        a_bf[:, z] = out[:, z].astype(jnp.bfloat16)

    row_loop(lambda peer: fwd_a(peer, 0, row).start())

    load_base.wait()

    @pl.loop(0, 3)
    def _(field):
        for z0 in range(0, nz, 16):
            z_src[field, :, z0 : z0 + 16, :] = jnp.swapaxes(
                out[field, z0 : z0 + 16], 0, 1
            ).astype(jnp.bfloat16)
            z_src[3 + field, :, z0 : z0 + 16, :] = jnp.swapaxes(
                base[field, z0 : z0 + 16].astype(jnp.float32), 0, 1
            ).astype(jnp.bfloat16)

    def send_y(chunk):
        def both(peer):
            fwd_a(peer, chunk, row).start()
            fwd_u(peer, chunk, row).start()

        row_loop(both)

    if zc > 1:
        send_y(1)

    @pl.loop(0, zc)
    def _(part):
        col_loop(lambda peer: fwd_z(peer, part, col).start())

    def terms(adj, flow, own, derive, length, axis):
        half = flow[own].astype(jnp.float32)
        transfer = None
        for field in range(3):
            part = adj[field].astype(jnp.float32) * derive(flow[field], False)
            transfer = part if transfer is None else transfer + part
        listing = []
        for field in range(3):
            both = derive(adj[field], True)
            first = lax.slice_in_dim(both, 0, length, axis=axis)
            second = lax.slice_in_dim(both, length, 2 * length, axis=axis)
            term = half * first + viscosity * second
            listing.append(term - transfer if field == own else term)
        return listing

    step = 4
    @pl.loop(0, nz // step)
    def _(part):
        planes = pl.ds(part * step, step)

        def derive(lines, both):
            matrix = stream[...] if both else stream[:nx]
            return lax.dot_general(
                lines, matrix, (((1,), (1,)), ((), ())), preferred_element_type=jnp.float32
            )

        adj = [a_bf[field, planes].reshape(step * ny, nx) for field in range(3)]
        flow = [base[field, planes].reshape(step * ny, nx) for field in range(3)]
        for field, term in enumerate(terms(adj, flow, 0, derive, nx, 1)):
            out[field, planes] += section_step * term.reshape(step, ny, nx)

    def column_terms(matrix_ref, adj, flow, own):
        length = matrix_ref.shape[1]

        def derive(lines, both):
            matrix = matrix_ref[...] if both else matrix_ref[:length]
            return jnp.dot(matrix, lines, preferred_element_type=jnp.float32)

        return terms(adj, flow, own, derive, length, 0)

    @pl.loop(0, zc)
    def _(chunk):
        for field in range(3):
            y_a[field, chunk, y_rows(row), :] = a_bf[field, row * zc + chunk]
            y_u[field, chunk, y_rows(row), :] = base[field, row * zc + chunk]

    @pl.loop(0, yc)
    def _(line):
        for field in range(6):
            z_recv[field, line, z_rows(col), :] = z_src[field, col * yc + line]

    def y_chunk(chunk):
        @pl.loop(1, rows)
        def _(offset):
            source = row_at(offset)
            fwd_a(source, chunk, source).wait_recv()
            fwd_u(source, chunk, source).wait_recv()

        @pl.when(chunk + 2 < zc)
        def _():
            send_y(chunk + 2)

        adj = [y_a[field, chunk] for field in range(3)]
        flow = [y_u[field, chunk] for field in range(3)]
        for field, term in enumerate(column_terms(normal, adj, flow, 1)):
            y_term[field, chunk] = term.astype(jnp.bfloat16)

        row_loop(lambda peer: back_y(peer, chunk, row).start())
        own_y(chunk).start()

    def z_part(part):
        col_loop(lambda source: fwd_z(source, part, source).wait_recv())

        @pl.loop(0, yp)
        def _(step):
            line = part * yp + step
            adj = [z_recv[field, line] for field in range(3)]
            flow = [z_recv[3 + field, line] for field in range(3)]
            for field, term in enumerate(column_terms(span, adj, flow, 2)):
                z_term[field, line] = term.astype(jnp.bfloat16)

        col_loop(lambda peer: back_z(peer, part, col).start())

        @pl.loop(0, yp)
        def _(step):
            line = part * yp + step
            for field in range(3):
                z_back[field, col * yc + line] = z_term[field, line, z_rows(col), :]

    @pl.loop(0, zc)
    def _(chunk):
        y_chunk(chunk)
        z_part(chunk)

    @pl.loop(0, zc)
    def _(part):
        col_loop(lambda source: back_z(source, part, source).wait_recv())

    @pl.loop(0, 3)
    def _(field):
        for z0 in range(0, nz, 16):
            out[field, z0 : z0 + 16] += section_step * jnp.swapaxes(
                z_back[field, :, z0 : z0 + 16, :].astype(jnp.float32), 0, 1
            )

    store = pltpu.make_async_copy(out, out_hbm, load_sem.at[0])
    store.start()

    @pl.loop(0, zc)
    def _(chunk):
        own_y(chunk).wait()

        @pl.loop(1, rows)
        def _(offset):
            source = row_at(offset)
            back_y(source, chunk, source).wait_recv()

    store.wait()

    @pl.loop(0, zc)
    def _(chunk):
        @pl.loop(1, rows)
        def _(offset):
            peer = row_at(offset)
            fwd_a(peer, chunk, row).wait_send()
            fwd_u(peer, chunk, row).wait_send()
            back_y(peer, chunk, row).wait_send()

    @pl.loop(0, zc)
    def _(part):
        @pl.loop(1, cols)
        def _(offset):
            peer = col_at(offset)
            fwd_z(peer, part, col).wait_send()
            back_z(peer, part, col).wait_send()


def local_kernel(adjoint, base_flow, stream_pair, normal_pair, span_pair):
    rows = lax.axis_size("rows")
    cols = lax.axis_size("cols")
    _, nz, ny, nx = adjoint.shape
    zc, yc = nz // rows, ny // cols
    bf = jnp.bfloat16
    vmem = pl.BlockSpec(memory_space=pltpu.VMEM)
    row_sems = [pltpu.SemaphoreType.DMA((zc, rows))] * 6
    col_sems = [pltpu.SemaphoreType.DMA((zc, cols))] * 4
    far = pl.BlockSpec(memory_space=pl.ANY)
    partial, y_terms = pl.pallas_call(
        functools.partial(section_kernel, rows, cols),
        out_shape=(
            jax.ShapeDtypeStruct(adjoint.shape, jnp.float32),
            jax.ShapeDtypeStruct(adjoint.shape, bf),
        ),
        in_specs=[far, far, vmem, vmem, vmem],
        out_specs=(far, far),
        scratch_shapes=[
            pltpu.VMEM((3, nz, ny, nx), jnp.float32),
            pltpu.VMEM((3, nz, ny, nx), bf),
            pltpu.VMEM((3, nz, ny, nx), bf),
            pltpu.VMEM((3, zc, rows * ny, nx), bf),
            pltpu.VMEM((3, zc, rows * ny, nx), bf),
            pltpu.VMEM((6, ny, nz, nx), bf),
            pltpu.VMEM((6, yc, cols * nz, nx), bf),
            pltpu.VMEM((3, zc, rows * ny, nx), bf),
            pltpu.VMEM((3, yc, cols * nz, nx), bf),
            pltpu.VMEM((3, ny, nz, nx), bf),
            *row_sems,
            *col_sems,
            pltpu.SemaphoreType.DMA((zc,)),
            pltpu.SemaphoreType.DMA((2,)),
        ],
        compiler_params=pltpu.CompilerParams(
            collective_id=0, has_side_effects=True, vmem_limit_bytes=60 * 1024 * 1024
        ),
    )(adjoint, base_flow, stream_pair, normal_pair, span_pair)
    return partial + section_step * y_terms.astype(jnp.float32)


def section(adjoint, base_flow, stream_pair, normal_pair, span_pair):
    _, nz, ny, nx = adjoint.shape
    rows, cols = lax.axis_size("rows"), lax.axis_size("cols")
    whole = nz % 16 == 0 and ny % 16 == 0 and nx % 128 == 0
    if whole and rows % 2 == 0 and nz % rows == 0 and ny % (cols * (nz // rows)) == 0:
        return local_kernel(adjoint, base_flow, stream_pair, normal_pair, span_pair)
    return local(adjoint, base_flow, stream_pair, normal_pair, span_pair)


def solution(mesh):
    placed = (P(None, "cols", "rows", None), P(None, "cols", "rows", None), P(), P(), P())
    return jax.shard_map(
        section, mesh=mesh, in_specs=placed, out_specs=P(None, "cols", "rows", None), check_vma=False
    )
```
